32 devices in a mesh: groups: 2 (over y), owner: 8 (over z, core), tp: 2 (over x).
Axes of the slice: x: 2, y: 2, z: 4, core: 2. Of those that a mesh axis runs over, the one named last changes fastest.
Arguments:
- tokens: bfloat16 [8192, 8192], P(('groups', 'owner'), 'tp'), parts along dimension 0, may hold values from -6 to 6
- base_value_weight: bfloat16 [8192, 1024], P(('tp', 'owner')), may hold values from -0.0625 to 0.0625
- adapter_down_factor: bfloat16 [8, 8192, 64], P(None, ('tp', 'owner')), may hold values from -0.0625 to 0.0625
- adapter_up_factor: bfloat16 [8, 64, 1024], P(None, 'owner', 'tp'), may hold values from -0.75 to 0.75
- relevance_weight: float32 [1024], P('tp'), may hold values from -0.1875 to 0.1875
- tile_adapter_index: int32 [64], P(('groups', 'owner')), parts along dimension 0, may hold values from 0 to 7
- adapter_storage_slot: int32 [8], replicated, may hold values from 0 to 7, each once
- tile_live_length: int32 [64], P(('groups', 'owner')), parts along dimension 0, may hold values from 1 to 128, 3072 in all
- passage_document: int32 [64], P(('groups', 'owner')), parts along dimension 0, may hold values from 0 to 15, never falling along the last dimension, each value on 1 to 4 neighbouring positions
- document_output_slot: int32 [32], P('groups'), parts along dimension 0, may hold values from 0 to 15, each once
Outputs:
- values: bfloat16 [8192, 1024], P(('groups', 'owner'), 'tp'), parts along dimension 0
- doc_scores: float32 [32], P(('groups', 'owner')), parts along dimension 0
The draws below stay inside these ranges and needn't reach their ends.
There are 2 independent parts, one for each index of `groups`. The reference program is written for one: setup_inputs(seed, part) draws one part's arguments, and reference() takes and returns one part's arrays. A program takes and returns all parts, laid end to end along the dimension named above; an argument that names none is the same for every part. Nothing has to cross between parts.
All inputs are finite; a program needn't handle non-finite values. No bound on the sum of `tile_live_length` on one device may be relied on, other than what follows from the above.
Results may differ from the reference program's by a relative error of at most 0.0039.
Values may be sent and summed in bfloat16 or wider, within the bound.
A program may use at most 64 MiB of HBM per device.

```python
import math
import jax
import jax.numpy as jnp
import numpy as np
from jax import lax

MODEL_WIDTH = 8192
VALUE_WIDTH = 1024
ADAPTER_RANK = 64
TILE = 128
TILES = 32
TOKENS = 4096
ADAPTER_TOTAL = 8
DOCS = 16


def plant(values, stream_key, smallest, high):
    place = [jax.random.randint(jax.random.fold_in(stream_key, axis), (), 0, length) for axis, length in enumerate(values.shape)]
    widest = values.shape.index(max(values.shape))
    beside = place[:widest] + [(place[widest] + 1) % values.shape[widest]] + place[widest + 1:]
    return values.at[tuple(place)].set(smallest).at[tuple(beside)].set(high)


def block_scale(rng, shape, cuts, low, largest):
    factor_of, own = 1.0, jax.random.fold_in(rng, 6)
    for axis_at, shards_of in cuts:
        steps = jnp.exp(jax.random.uniform(jax.random.fold_in(own, axis_at), (shards_of,), jnp.float32, low / len(cuts), largest / len(cuts)))
        factor_of = factor_of * jnp.repeat(steps, shape[axis_at] // shards_of).reshape([-1 if axis == axis_at else 1 for axis in range(len(shape))])
    return factor_of


def rank_bounds(amount, lean):
    portions = [(1 << 20) // math.isqrt(standing ** lean) + 1 for standing in range(1, amount + 1)]
    width = 1 + sum(portions) // (1 << 30)
    return np.cumsum(np.array([max(1, weight // width) for weight in portions]))


def ranked(key, shape, count, slope):
    listing = rank_bounds(count, slope)
    lot = jax.random.randint(jax.random.fold_in(key, 1), shape, 0, int(listing[count - 1]))
    standing = jnp.searchsorted(jnp.asarray(listing, jnp.int32), lot, side="right")
    return jax.random.permutation(jax.random.fold_in(key, 2), count)[standing].astype(jnp.int32)


def split_up(amount, total, most, lean):
    loads = [(1 << 20) // math.isqrt(standing ** lean) + 1 for standing in range(2, amount + 1)]
    rest, counts = total - most - (amount - 1), [1] * (amount - 1)
    while rest > 0:
        free = [i for i in range(amount - 1) if counts[i] < most]
        whole, budget = sum([loads[i] for i in free]), rest
        for i in free:
            addition = min(most - counts[i], max(1, budget * loads[i] // whole), rest)
            counts[i] = counts[i] + addition
            rest = rest - addition
    return np.array([most] + counts)


def uneven(rng, number_of, total, limit, skew):
    if number_of == 2:
        one = jax.random.randint(rng, (), max(1, total - limit), min(limit, total - 1) + 1)
        return jnp.stack([one, total - one])
    tallies = jnp.asarray(split_up(number_of, total, limit, skew), jnp.int32)
    pairs = (number_of - 1) // 2
    giver, taker = tallies[1:1 + 2 * pairs:2], tallies[2:2 + 2 * pairs:2]
    room = jnp.minimum(giver - 1, limit - taker)
    shifted = jax.random.randint(jax.random.fold_in(rng, 1), (pairs,), 0, 1 << 20) % (room + 1)
    tallies = tallies.at[1:1 + 2 * pairs:2].set(giver - shifted).at[2:2 + 2 * pairs:2].set(taker + shifted)
    return tallies[jax.random.permutation(jax.random.fold_in(rng, 2), number_of)]


def gaussian(rng, extent, scale, bound, shards=(), kind=jnp.bfloat16):
    factor_of = block_scale(rng, extent, shards, -0.22, 0.18) if shards else 1.0
    drawn = jax.random.normal(rng, extent, jnp.float32) * scale * factor_of
    return jnp.minimum(jnp.maximum(drawn, -bound), bound).astype(kind)


def setup_inputs(seed: int = 0, part: int = 0) -> dict:
    keys = jax.random.split(jax.random.key(seed), 11)
    part_keys = jax.random.split(jax.random.fold_in(keys[10], part), 11)
    return {
        "tokens": gaussian(part_keys[0], (TOKENS, MODEL_WIDTH), 1.0, 6.0, ((0, 8), (1, 2))),
        "base_value_weight": gaussian(keys[1], (MODEL_WIDTH, VALUE_WIDTH), MODEL_WIDTH ** -0.5, 0.0625, ((0, 16),)),
        "adapter_down_factor": gaussian(keys[2], (ADAPTER_TOTAL, MODEL_WIDTH, ADAPTER_RANK), MODEL_WIDTH ** -0.5, 0.0625, ((1, 16),)),
        "adapter_up_factor": gaussian(keys[3], (ADAPTER_TOTAL, ADAPTER_RANK, VALUE_WIDTH), ADAPTER_RANK ** -0.5, 0.75, ((1, 8), (2, 2))),
        "relevance_weight": gaussian(keys[4], (VALUE_WIDTH,), VALUE_WIDTH ** -0.5, 0.1875, ((0, 2),), jnp.float32),
        "tile_adapter_index": plant(ranked(part_keys[5], (TILES,), ADAPTER_TOTAL, 2), jax.random.fold_in(part_keys[5], 3), 0, ADAPTER_TOTAL - 1).astype(jnp.int32),
        "adapter_storage_slot": jax.random.permutation(keys[6], ADAPTER_TOTAL).astype(jnp.int32),
        "tile_live_length": uneven(part_keys[7], TILES, TILES * TILE * 3 // 4, TILE, 1).astype(jnp.int32),
        "passage_document": jnp.searchsorted(jnp.cumsum(uneven(part_keys[8], DOCS, TILES, 4, 1)), jnp.arange(TILES), side="right").astype(jnp.int32),
        "document_output_slot": jax.random.permutation(part_keys[9], DOCS).astype(jnp.int32),
    }


def reference(tokens, base_value_weight, adapter_down_factor, adapter_up_factor, relevance_weight, tile_adapter_index, adapter_storage_slot, tile_live_length, passage_document, document_output_slot):
    slots = lax.optimization_barrier(jnp.sum(jnp.where(tile_adapter_index[:, None] == jnp.arange(ADAPTER_TOTAL, dtype=jnp.int32)[None, :], adapter_storage_slot[None, :], 0), axis=1)).astype(jnp.int32)
    base = jnp.dot(tokens, base_value_weight, preferred_element_type=jnp.float32)
    tiled_tokens = tokens.reshape(TILES, TILE, MODEL_WIDTH)

    def one_tile(pair):
        value_block, storage_index = pair
        low_rank_term = jnp.dot(value_block, adapter_down_factor[storage_index], preferred_element_type=jnp.float32).astype(jnp.bfloat16)
        return jnp.dot(low_rank_term, adapter_up_factor[storage_index], preferred_element_type=jnp.float32)
    delta = lax.map(one_tile, (tiled_tokens, slots)).reshape(TOKENS, VALUE_WIDTH)
    adapted = base + delta
    values = adapted.astype(jnp.bfloat16)
    token_score = jnp.dot(jax.nn.silu(adapted), relevance_weight, precision=lax.Precision.HIGHEST).reshape(TILES, TILE)
    live = jnp.arange(TILE, dtype=jnp.int32)[None, :] < tile_live_length[:, None]
    passage = lax.optimization_barrier(jnp.sum(jnp.where(live, token_score, 0.0), axis=1)) / jnp.sqrt(tile_live_length.astype(jnp.float32))
    doc_slot = lax.optimization_barrier(jnp.sum(jnp.where(passage_document[:, None] == jnp.arange(DOCS, dtype=jnp.int32)[None, :], document_output_slot[None, :], 0), axis=1))
    doc_scores = lax.optimization_barrier(jnp.max(jnp.where(doc_slot[:, None] == jnp.arange(DOCS, dtype=jnp.int32)[None, :], passage[:, None], -1e+30), axis=0))
    return (values, doc_scores)
```

```python
import functools

import jax
import jax.numpy as jnp
from jax import lax
from jax.experimental import pallas as pl
from jax.experimental.pallas import tpu as pltpu
from jax.sharding import PartitionSpec as P

TILE = 128
CORES = 2
LOWEST = -1e30
MESH = pl.DeviceIdType.MESH
F32 = jnp.float32
BF16 = jnp.bfloat16


class Plan:
    def __init__(self, n_owner, n_tp, tokens, weight, down, up, docs):
        self.n_owner, self.n_tp = n_owner, n_tp
        self.nz = n_owner // CORES
        self.tok, self.feat = tokens.shape
        self.tiles = self.tok // TILE
        self.rows = weight.shape[0]
        self.cols = weight.shape[1] // n_tp
        self.adapters, _, self.rank = down.shape
        self.wide = self.adapters * self.rank
        self.rank_rows = up.shape[1]
        self.up_rows = self.adapters * self.rank_rows
        self.docs = docs
        self.doc_dev = docs // n_owner
        self.lanes = -(-docs // 128) * 128
        self.flat = self.rows % 128 == 0
        self.parts_w = 2 if self.rows >= 256 else 1
        self.groups = list(range(n_tp - 1)) + ["d", n_tp - 1]
        self.part_of, self.parts = {}, 0
        for g in self.groups:
            count = 2 if g == "d" else self.parts_w
            self.part_of[g] = list(range(self.parts, self.parts + count))
            self.parts += count


def kernel(
    p,
    tok_hbm, w_hbm, d_hbm, u_hbm, rel_ref, tile_adapter, storage, live, passage_doc, doc_slot,
    out_hbm, score_ref,
    tok, wbuf, dbuf, ubuf, acc, low, low_in, sums_in, term, out, marks,
    load_sem, z_recv, y_recv, c_recv, up_send, down_send, y_send, c_send,
    x_send, x_recv, l_send, l_recv, m_send, m_recv, out_sem,
):
    gi, owner, tp = lax.axis_index("groups"), lax.axis_index("owner"), lax.axis_index("tp")
    zi, ci = owner // CORES, owner % CORES
    devices = p.n_tp * p.n_owner
    me = tp * p.n_owner + owner

    barrier = pltpu.get_barrier_semaphore()

    def greet(k, carry):
        peer = lax.rem(me + k, devices)
        pl.semaphore_signal(
            barrier, inc=1, device_id={"tp": peer // p.n_owner, "owner": lax.rem(peer, p.n_owner)},
            device_id_type=MESH,
        )
        return carry

    lax.fori_loop(1, devices, greet, 0)
    pl.semaphore_signal(barrier, inc=1, device_id={"groups": 1 - gi}, device_id_type=MESH)

    def columns(g):
        t = lax.rem(tp + 1 + g, p.n_tp)
        return pl.ds(pl.multiple_of(t * p.cols, 128), p.cols)

    own_rows = pl.ds(pl.multiple_of(owner * p.rows, p.rows), p.rows)
    loads = []
    for g in p.groups:
        if g == "d":
            there = dbuf.at[owner] if p.flat else dbuf.at[own_rows]
            loads.append((d_hbm, there))
            loads.append((u_hbm, ubuf.at[pl.ds(pl.multiple_of(owner * p.up_rows, p.up_rows), p.up_rows)]))
        else:
            loads.append((w_hbm.at[:, columns(g)], wbuf.at[g, own_rows]))
    loads.append((tok_hbm, tok))
    loads = [pltpu.make_async_copy(a, b, load_sem.at[i]) for i, (a, b) in enumerate(loads)]
    for load in loads:
        load.start()
    for load in loads[:-1]:
        load.wait()
    pl.semaphore_wait(barrier, devices)

    def piece(part, z, c, h):
        o = z * CORES + c
        for g in p.groups:
            if part in p.part_of[g]:
                k = p.part_of[g].index(part)
                break
        if g == "d":
            if k == 1:
                half = p.up_rows // 2
                return ubuf.at[pl.ds(pl.multiple_of(o * p.up_rows + h * half, half), half)]
            if p.flat:
                half = p.wide // 2
                return dbuf.at[o, pl.ds(pl.multiple_of(h * half, half), half)]
            half = p.rows // 2
            return dbuf.at[pl.ds(pl.multiple_of(o * p.rows + h * half, half), half)]
        half = p.rows // 2
        size = half // p.parts_w
        return wbuf.at[g, pl.ds(pl.multiple_of(o * p.rows + h * half + k * size, size), size)]

    def send(part, z, c, h, send_sem, recv_sem, device):
        ref = piece(part, z, c, h)
        return pltpu.make_async_remote_copy(
            src_ref=ref, dst_ref=ref, send_sem=send_sem, recv_sem=recv_sem,
            device_id=device, device_id_type=MESH,
        )

    def up(part, z):
        return send(part, z, ci, gi, up_send.at[part, z], z_recv.at[part, z],
                    {"owner": lax.rem(owner + CORES, p.n_owner)})

    def down(part, z):
        return send(part, z, ci, gi, down_send.at[part, z], z_recv.at[part, z],
                    {"owner": lax.rem(owner + p.n_owner - CORES, p.n_owner)})

    def across(part, z, h=None):
        return send(part, z, ci, gi if h is None else h, y_send.at[part, z], y_recv.at[part, z],
                    {"groups": 1 - gi})

    def beside(part, z, c, h):
        return send(part, z, c, h, c_send.at[part, z, h], c_recv.at[part, z, h],
                    {"owner": zi * CORES + 1 - ci})

    def own_sends(g):
        for part in p.part_of[g]:
            @pl.when(zi + 1 < p.nz)
            def _():
                up(part, zi).start()

            @pl.when(zi > 0)
            def _():
                down(part, zi).start()
            for h in range(2):
                beside(part, zi, ci, h).start()

    def each_way(s, body):
        @pl.when(zi - s >= 0)
        def _():
            body(zi - s, True)

        @pl.when(zi + s < p.nz)
        def _():
            body(zi + s, False)

    def stage_z(g, s):
        def body(z, upward):
            for part in p.part_of[g]:
                up(part, z).wait_recv()
                if upward:
                    @pl.when(zi + 1 < p.nz)
                    def _():
                        up(part, z).start()
                else:
                    @pl.when(zi > 0)
                    def _():
                        down(part, z).start()
                across(part, z).start()
                beside(part, z, ci, gi).start()
        each_way(s, body)

    def stage_y(g, s):
        def body(z, upward):
            for part in p.part_of[g]:
                across(part, z, 1 - gi).wait_recv()
                beside(part, z, ci, 1 - gi).start()
        each_way(s, body)

    def slot_of(g):
        return p.n_tp if g == "d" else g

    def add_block(g, z, first):
        span = CORES * p.rows
        rows = TILE

        def body(j, carry):
            r = pl.ds(pl.multiple_of(j * rows, rows), rows)
            if g == "d":
                total = None
                for c in range(CORES):
                    f = pl.ds(pl.multiple_of(z * span + c * p.rows, 128), p.rows)
                    part = lax.dot_general(tok[r, f], dbuf[z * CORES + c], (((1,), (1,)), ((), ())),
                                           preferred_element_type=F32)
                    total = part if total is None else total + part
                low[r] = total if first else low[r] + total
            else:
                f = pl.ds(pl.multiple_of(z * span, 128), span)
                k = pl.ds(pl.multiple_of(z * span, span), span)
                part = jnp.dot(tok[r, f], wbuf[g, k], preferred_element_type=F32)
                acc[g, r] = part if first else acc[g, r] + part
            return carry

        lax.fori_loop(0, p.tiles, body, 0)

    def all_blocks(g):
        def body(j, carry):
            r = pl.ds(pl.multiple_of(j * TILE, TILE), TILE)
            if g == "d":
                low[r] = jnp.dot(tok[r], dbuf[...], preferred_element_type=F32)
            else:
                acc[g, r] = jnp.dot(tok[r], wbuf[g], preferred_element_type=F32)
            return carry

        lax.fori_loop(0, p.tiles, body, 0)

    def stage_c(g, s):
        def body(z, upward):
            for part in p.part_of[g]:
                for h in range(2):
                    beside(part, z, 1 - ci, h).wait_recv()
            if p.flat:
                add_block(g, z, s == 0)
        if s == 0:
            body(zi, True)
        else:
            each_way(s, body)

    def to_tp(ref_src, ref_dst, k, s_sem, r_sem):
        return pltpu.make_async_remote_copy(
            src_ref=ref_src, dst_ref=ref_dst, send_sem=s_sem.at[k], recv_sem=r_sem.at[k],
            device_id={"tp": lax.rem(tp + 1 + k, p.n_tp)}, device_id_type=MESH,
        )

    def sums_copy(k):
        return to_tp(acc.at[k], sums_in.at[k], k, x_send, x_recv)

    def low_copy(k):
        return to_tp(low_in.at[p.n_tp - 1], low_in.at[k], k, l_send, l_recv)

    def slot_at(j):
        return storage[tile_adapter[j]]

    def pick_low():
        def body(j, carry):
            r = pl.ds(pl.multiple_of(j * TILE, TILE), TILE)
            slot = slot_at(j)
            lane = lax.broadcasted_iota(jnp.int32, (TILE, 128), 1)
            total = jnp.zeros((TILE, 128), F32)
            for pair in range(p.wide // 128):
                here = (pair * 128 + lane) // p.rank == slot
                total = total + jnp.where(here, low[r, pair * 128:(pair + 1) * 128], 0.0)
            low_in[p.n_tp - 1, r] = total
            return carry

        lax.fori_loop(0, p.tiles, body, 0)

    def finish(g):
        if not p.flat:
            all_blocks(g)
        if g == "d":
            pick_low()
            for k in range(p.n_tp - 1):
                low_copy(k).start()
        elif g < p.n_tp - 1:
            sums_copy(g).start()

    def adapter_term():
        for k in range(p.n_tp - 1):
            low_copy(k).wait_recv()
        row = lax.broadcasted_iota(jnp.int32, (128, p.wide), 0) % p.rank
        col = lax.broadcasted_iota(jnp.int32, (128, p.wide), 1)
        rank_of = (col // p.up_rows) * p.rank_rows + col % p.rank_rows
        spread = jnp.where(row == rank_of, 1.0, 0.0).astype(BF16)

        def body(j, carry):
            r = pl.ds(pl.multiple_of(j * TILE, TILE), TILE)
            slot = slot_at(j)
            total = low_in[p.n_tp - 1, r]
            for k in range(p.n_tp - 1):
                total = total + low_in[k, r]
            laid = jnp.dot(total.astype(BF16), spread, preferred_element_type=F32)
            lane = lax.broadcasted_iota(jnp.int32, (TILE, p.wide), 1)
            here = (lane // p.rank_rows) % p.adapters == slot
            laid = jnp.where(here, laid, 0.0).astype(BF16)
            term[r] = jnp.dot(laid, ubuf[...], preferred_element_type=F32)
            return carry

        lax.fori_loop(0, p.tiles, body, 0)

    steps = [(g, s) for g in p.groups for s in range(p.nz)]
    own_sends(p.groups[0])
    loads[-1].wait()
    for i in range(len(steps) + 2):
        if i < len(steps):
            g, s = steps[i]
            if s == 0:
                after = p.groups.index(g) + 1
                if after < len(p.groups):
                    own_sends(p.groups[after])
            else:
                stage_z(g, s)
        if 1 <= i <= len(steps):
            g, s = steps[i - 1]
            if s > 0:
                stage_y(g, s)
        if i == len(steps) - 1:
            c_before = steps[i - 2]
            stage_c(*c_before)
            if c_before[1] == p.nz - 1:
                finish(c_before[0])
            adapter_term()
        elif i >= 2:
            g, s = steps[i - 2]
            stage_c(g, s)
            if s == p.nz - 1:
                finish(g)

    for k in range(p.n_tp - 1):
        sums_copy(k).wait_recv()
    marks[me] = jnp.full((marks.shape[1], p.lanes), jnp.where(tp == 0, LOWEST, 0.0), F32)
    weight = rel_ref[...]

    def tile_out(j):
        r = pl.ds(pl.multiple_of(j * TILE, TILE), TILE)
        return pltpu.make_async_copy(out.at[r], out_hbm.at[r], out_sem.at[j])

    def last(j, carry):
        r = pl.ds(pl.multiple_of(j * TILE, TILE), TILE)
        adapted = acc[p.n_tp - 1, r]
        for k in range(p.n_tp - 1):
            adapted = adapted + sums_in[k, r]
        adapted = adapted + term[r]
        out[r] = adapted.astype(BF16)
        tile_out(j).start()
        scored = adapted / (1.0 + jnp.exp(-adapted)) * weight
        length = live[j]
        token = lax.broadcasted_iota(jnp.int32, scored.shape, 0)
        scored = jnp.where(token < length, scored, 0.0)
        part = jnp.sum(jnp.sum(scored, axis=0, keepdims=True), axis=1, keepdims=True)
        scale = jnp.sqrt(jnp.full((1, p.lanes), length, jnp.int32).astype(F32))
        slot = doc_slot[passage_doc[j]]
        lane = lax.broadcasted_iota(jnp.int32, (1, p.lanes), 1)
        empty = jnp.where(tp == 0, LOWEST, 0.0)
        marks[me, pl.ds(j, 1)] = jnp.where(lane == slot, part / scale, empty)
        return carry

    lax.fori_loop(0, p.tiles, last, 0)

    def mark_copy(k, slot, sender):
        peer = lax.rem(me + k, devices)
        return pltpu.make_async_remote_copy(
            src_ref=marks.at[slot], dst_ref=marks.at[slot], send_sem=m_send.at[k], recv_sem=m_recv.at[sender],
            device_id={"tp": peer // p.n_owner, "owner": lax.rem(peer, p.n_owner)}, device_id_type=MESH,
        )

    def mark_start(k, carry):
        mark_copy(k, me, me).start()
        return carry

    def mark_wait(k, carry):
        sender = lax.rem(me + k, devices)
        mark_copy(k, sender, sender).wait_recv()
        return carry

    def mark_sent(k, carry):
        mark_copy(k, me, me).wait_send()
        return carry

    lax.fori_loop(1, devices, mark_start, 0)

    for g in p.groups:
        for part in p.part_of[g]:
            for s in range(p.nz):
                def gone(z, upward):
                    if upward:
                        @pl.when(zi + 1 < p.nz)
                        def _():
                            up(part, z).wait_send()
                    if s == 0 or not upward:
                        @pl.when(zi > 0)
                        def _():
                            down(part, z).wait_send()
                    if s > 0:
                        across(part, z).wait_send()
                    for h in range(2):
                        beside(part, z, ci, h).wait_send()
                if s == 0:
                    gone(zi, True)
                else:
                    each_way(s, gone)
    for k in range(p.n_tp - 1):
        sums_copy(k).wait_send()
        low_copy(k).wait_send()

    lax.fori_loop(1, devices, mark_wait, 0)
    best = None
    for o in range(p.n_owner):
        total = marks[o]
        for t in range(1, p.n_tp):
            total = total + marks[t * p.n_owner + o]
        best = total if best is None else jnp.maximum(best, total)
    lane = lax.broadcasted_iota(jnp.int32, best.shape, 1)
    for d in range(p.doc_dev):
        score_ref[d] = jnp.max(jnp.where(lane == owner * p.doc_dev + d, best, 2 * LOWEST))

    lax.fori_loop(1, devices, mark_sent, 0)

    def out_wait(j, carry):
        tile_out(j).wait()
        return carry

    lax.fori_loop(0, p.tiles, out_wait, 0)


def shards(
    n_owner, n_tp,
    tokens,
    base_value_weight,
    adapter_down_factor,
    adapter_up_factor,
    relevance_weight,
    tile_adapter_index,
    adapter_storage_slot,
    tile_live_length,
    passage_document,
    document_output_slot,
):
    p = Plan(
        n_owner, n_tp, tokens, base_value_weight, adapter_down_factor, adapter_up_factor,
        document_output_slot.shape[0],
    )
    if p.flat:
        down = jnp.transpose(adapter_down_factor, (0, 2, 1)).reshape(p.wide, p.rows)
        dshape = (p.n_owner, p.wide, p.rows)
    else:
        down = jnp.transpose(adapter_down_factor, (1, 0, 2)).reshape(p.rows, p.wide)
        dshape = (p.feat, p.wide)
    up = adapter_up_factor.reshape(p.up_rows, p.cols)
    peers = max(1, p.n_tp - 1)
    devices = p.n_tp * p.n_owner
    dma = pltpu.SemaphoreType.DMA
    mark_rows = -(-p.tiles // 8) * 8
    hbm, smem = pl.BlockSpec(memory_space=pl.ANY), pl.BlockSpec(memory_space=pltpu.SMEM)
    return pl.pallas_call(
        functools.partial(kernel, p),
        out_shape=(
            jax.ShapeDtypeStruct((p.tok, p.cols), BF16),
            jax.ShapeDtypeStruct((p.doc_dev,), F32),
        ),
        in_specs=[hbm] * 4 + [pl.BlockSpec(memory_space=pltpu.VMEM)] + [smem] * 5,
        out_specs=(hbm, smem),
        scratch_shapes=[
            pltpu.VMEM((p.tok, p.feat), BF16),
            pltpu.VMEM((p.n_tp, p.feat, p.cols), BF16),
            pltpu.VMEM(dshape, BF16),
            pltpu.VMEM((p.wide, p.cols), BF16),
            pltpu.VMEM((p.n_tp, p.tok, p.cols), F32),
            pltpu.VMEM((p.tok, p.wide), F32),
            pltpu.VMEM((p.n_tp, p.tok, 128), F32),
            pltpu.VMEM((peers, p.tok, p.cols), F32),
            pltpu.VMEM((p.tok, p.cols), F32),
            pltpu.VMEM((p.tok, p.cols), BF16),
            pltpu.VMEM((devices, mark_rows, p.lanes), F32),
            dma((p.n_tp + 3,)),
            dma((p.parts, p.nz)),
            dma((p.parts, p.nz)),
            dma((p.parts, p.nz, 2)),
            dma((p.parts, p.nz)),
            dma((p.parts, p.nz)),
            dma((p.parts, p.nz)),
            dma((p.parts, p.nz, 2)),
            dma((peers,)),
            dma((peers,)),
            dma((peers,)),
            dma((peers,)),
            dma((devices,)),
            dma((devices,)),
            dma((p.tiles,)),
        ],
        compiler_params=pltpu.CompilerParams(
            collective_id=0, has_side_effects=True, vmem_limit_bytes=60 * 1024 * 1024
        ),
        name="gather_project_score",
    )(
        tokens, base_value_weight, down, up, relevance_weight.reshape(1, p.cols),
        tile_adapter_index, adapter_storage_slot, tile_live_length, passage_document, document_output_slot,
    )


def solution(mesh):
    placed = (
        P(("groups", "owner"), "tp"),
        P(("tp", "owner"), None),
        P(None, ("tp", "owner"), None),
        P(None, "owner", "tp"),
        P("tp"),
        P(("groups", "owner")),
        P(),
        P(("groups", "owner")),
        P(("groups", "owner")),
        P("groups"),
    )
    return jax.shard_map(
        functools.partial(shards, mesh.shape["owner"], mesh.shape["tp"]),
        mesh=mesh,
        in_specs=placed,
        out_specs=(P(("groups", "owner"), "tp"), P(("groups", "owner"))),
        check_vma=False,
    )
```

```python
import functools

import jax
import jax.numpy as jnp
from jax import lax
from jax.experimental import pallas as pl
from jax.experimental.pallas import tpu as pltpu
from jax.sharding import PartitionSpec as P

TILE = 128
CORES = 2
LOWEST = -1e30
LAGS = (1, 2)
MESH = pl.DeviceIdType.MESH
F32 = jnp.float32
BF16 = jnp.bfloat16


class Plan:
    def __init__(self, n_owner, n_tp, tokens, weight, down, up, docs):
        self.n_owner, self.n_tp = n_owner, n_tp
        self.nz = n_owner // CORES
        self.tok, self.feat = tokens.shape
        self.tiles = self.tok // TILE
        self.rows = weight.shape[0]
        self.cols = weight.shape[1] // n_tp
        self.adapters, _, self.rank = down.shape
        self.wide = self.adapters * self.rank
        self.rank_rows = up.shape[1]
        self.up_rows = self.adapters * self.rank_rows
        self.docs = docs
        self.doc_dev = docs // n_owner
        self.lanes = -(-docs // 128) * 128
        self.flat = self.rows % 128 == 0
        self.parts_w = {g: (4 if g == n_tp - 1 else 2) if self.rows >= 256 else 1 for g in range(n_tp)}
        self.parts_d = 2 if self.flat else 1
        self.whole = self.nz >= 4
        self.groups = list(range(n_tp - 1)) + ["d", n_tp - 1]
        self.part_of, self.parts = {}, 0
        for g in self.groups:
            count = self.parts_d + 1 if g == "d" else self.parts_w[g]
            self.part_of[g] = list(range(self.parts, self.parts + count))
            self.parts += count


def kernel(
    p,
    tok_hbm, w_hbm, d_hbm, u_hbm, rel_ref, tile_adapter, storage, live, passage_doc, doc_slot,
    out_hbm, score_ref,
    tok, wbuf, dbuf, ubuf, acc, low, low_in, sums_in, term, out, marks,
    load_sem, z_recv, y_recv, c_recv, e_recv, up_send, down_send, y_send, c_send, e_send,
    x_send, x_recv, l_send, l_recv, m_send, m_recv, out_sem,
):
    gi, owner, tp = lax.axis_index("groups"), lax.axis_index("owner"), lax.axis_index("tp")
    zi, ci = owner // CORES, owner % CORES
    devices = p.n_tp * p.n_owner
    me = tp * p.n_owner + owner

    barrier = pltpu.get_barrier_semaphore()

    def greet(**device):
        pl.semaphore_signal(barrier, inc=1, device_id=device, device_id_type=MESH)

    @pl.when(zi + 1 < p.nz)
    def _():
        greet(owner=lax.rem(owner + CORES, p.n_owner))

    @pl.when(zi > 0)
    def _():
        greet(owner=lax.rem(owner + p.n_owner - CORES, p.n_owner))

    greet(groups=1 - gi)
    greet(owner=zi * CORES + 1 - ci)
    for k in range(p.n_tp - 1):
        greet(tp=lax.rem(tp + 1 + k, p.n_tp))
    met = p.n_tp + 1 + jnp.where(zi > 0, 1, 0) + jnp.where(zi + 1 < p.nz, 1, 0)

    def columns(g):
        t = lax.rem(tp + 1 + g, p.n_tp)
        return pl.ds(pl.multiple_of(t * p.cols, 128), p.cols)

    own_rows = pl.ds(pl.multiple_of(owner * p.rows, p.rows), p.rows)
    loads, loads_of = [], {}
    for g in p.groups:
        loads_of[g] = [len(loads)] + ([len(loads) + 1] if g == "d" else [])
        if g == "d":
            there = dbuf.at[owner] if p.flat else dbuf.at[own_rows]
            loads.append((d_hbm, there))
            loads.append((u_hbm, ubuf.at[pl.ds(pl.multiple_of(owner * p.up_rows, p.up_rows), p.up_rows)]))
        else:
            loads.append((w_hbm.at[:, columns(g)], wbuf.at[g, own_rows]))
    loads.append((tok_hbm, tok))
    loads = [pltpu.make_async_copy(a, b, load_sem.at[i]) for i, (a, b) in enumerate(loads)]
    for load in loads:
        load.start()
    pl.semaphore_wait(barrier, met)

    def piece(part, z, c, h):
        o = z * CORES + c
        for g in p.groups:
            if part in p.part_of[g]:
                k = p.part_of[g].index(part)
                break
        if g == "d":
            if k == p.parts_d:
                half = p.up_rows // 2
                return ubuf.at[pl.ds(pl.multiple_of(o * p.up_rows + h * half, half), half)]
            if p.flat:
                half = p.wide // 2
                size = half // p.parts_d
                return dbuf.at[o, pl.ds(pl.multiple_of(h * half + k * size, size), size)]
            half = p.rows // 2
            return dbuf.at[pl.ds(pl.multiple_of(o * p.rows + h * half, half), half)]
        half = p.rows // 2
        size = half // p.parts_w[g]
        return wbuf.at[g, pl.ds(pl.multiple_of(o * p.rows + h * half + k * size, size), size)]

    def send(part, z, c, h, send_sem, recv_sem, device):
        ref = piece(part, z, c, h)
        return pltpu.make_async_remote_copy(
            src_ref=ref, dst_ref=ref, send_sem=send_sem, recv_sem=recv_sem,
            device_id=device, device_id_type=MESH,
        )

    def up(part, z):
        return send(part, z, ci, gi, up_send.at[part, z], z_recv.at[part, z],
                    {"owner": lax.rem(owner + CORES, p.n_owner)})

    def down(part, z):
        return send(part, z, ci, gi, down_send.at[part, z], z_recv.at[part, z],
                    {"owner": lax.rem(owner + p.n_owner - CORES, p.n_owner)})

    def across(part, z, h=None):
        return send(part, z, ci, gi if h is None else h, y_send.at[part, z], y_recv.at[part, z],
                    {"groups": 1 - gi})

    def beside(part, z, c, h):
        return send(part, z, c, h, c_send.at[part, z, h], c_recv.at[part, z, h],
                    {"owner": zi * CORES + 1 - ci})

    def extra(part, i):
        step = CORES if i == 0 else p.n_owner - CORES
        return send(part, zi, ci, 1 - gi, e_send.at[part, i], e_recv.at[part, i],
                    {"owner": lax.rem(owner + step, p.n_owner)})

    def extra_in(part, z, i):
        return send(part, z, ci, 1 - gi, e_send.at[part, i], e_recv.at[part, i], {"groups": 1 - gi})

    def own_sends(g):
        for i in loads_of[g]:
            loads[i].wait()
        for part in p.part_of[g]:
            @pl.when(zi + 1 < p.nz)
            def _():
                up(part, zi).start()

            @pl.when(zi > 0)
            def _():
                down(part, zi).start()
            for h in range(2):
                beside(part, zi, ci, h).start()
        if p.whole:
            for i, edge in enumerate((0, p.nz - 1)):
                @pl.when(zi == edge)
                def _():
                    for part in p.part_of[g]:
                        extra(part, i).start()

    def each_way(s, body):
        @pl.when(zi - s >= 0)
        def _():
            body(zi - s, True)

        @pl.when(zi + s < p.nz)
        def _():
            body(zi + s, False)

    def via_twin(s, upward, body, other=None):
        if not (p.whole and s == 1):
            body()
            return
        straight = zi == (1 if upward else p.nz - 2)

        @pl.when(jnp.logical_not(straight))
        def _():
            body()
        if other is not None:
            @pl.when(straight)
            def _():
                other()

    def stage_z(g, s):
        def body(z, upward):
            for part in p.part_of[g]:
                up(part, z).wait_recv()
                if upward:
                    @pl.when(zi + 1 < p.nz)
                    def _():
                        up(part, z).start()
                else:
                    @pl.when(zi > 0)
                    def _():
                        down(part, z).start()
                via_twin(s, upward, across(part, z).start)
                beside(part, z, ci, gi).start()
        each_way(s, body)

    def stage_y(g, s):
        def body(z, upward):
            for part in p.part_of[g]:
                via_twin(s, upward, lambda: across(part, z, 1 - gi).wait_recv(),
                         lambda: extra_in(part, z, 0 if upward else 1).wait_recv())
                beside(part, z, ci, 1 - gi).start()
        each_way(s, body)

    def slot_of(g):
        return p.n_tp if g == "d" else g

    def add_block(g, z, first):
        span = CORES * p.rows
        rows = TILE

        def body(j, carry):
            r = pl.ds(pl.multiple_of(j * rows, rows), rows)
            if g == "d":
                total = None
                for c in range(CORES):
                    f = pl.ds(pl.multiple_of(z * span + c * p.rows, 128), p.rows)
                    part = lax.dot_general(tok[r, f], dbuf[z * CORES + c], (((1,), (1,)), ((), ())),
                                           preferred_element_type=F32)
                    total = part if total is None else total + part
                low[r] = total if first else low[r] + total
            else:
                f = pl.ds(pl.multiple_of(z * span, 128), span)
                k = pl.ds(pl.multiple_of(z * span, span), span)
                part = jnp.dot(tok[r, f], wbuf[g, k], preferred_element_type=F32)
                acc[g, r] = part if first else acc[g, r] + part
            return carry

        lax.fori_loop(0, p.tiles, body, 0)

    def all_blocks(g):
        def body(j, carry):
            r = pl.ds(pl.multiple_of(j * TILE, TILE), TILE)
            if g == "d":
                low[r] = jnp.dot(tok[r], dbuf[...], preferred_element_type=F32)
            else:
                acc[g, r] = jnp.dot(tok[r], wbuf[g], preferred_element_type=F32)
            return carry

        lax.fori_loop(0, p.tiles, body, 0)

    def stage_c(g, s):
        def body(z, upward):
            for part in p.part_of[g]:
                for h in range(2):
                    beside(part, z, 1 - ci, h).wait_recv()
            if p.flat:
                add_block(g, z, s == 0)
        if s == 0:
            body(zi, True)
        else:
            each_way(s, body)

    def to_tp(ref_src, ref_dst, k, s_sem, r_sem):
        return pltpu.make_async_remote_copy(
            src_ref=ref_src, dst_ref=ref_dst, send_sem=s_sem.at[k], recv_sem=r_sem.at[k],
            device_id={"tp": lax.rem(tp + 1 + k, p.n_tp)}, device_id_type=MESH,
        )

    def sums_copy(k):
        return to_tp(acc.at[k], sums_in.at[k], k, x_send, x_recv)

    def low_copy(k):
        return to_tp(low_in.at[p.n_tp - 1], low_in.at[k], k, l_send, l_recv)

    def slot_at(j):
        return storage[tile_adapter[j]]

    def pick_low():
        def body(j, carry):
            r = pl.ds(pl.multiple_of(j * TILE, TILE), TILE)
            slot = slot_at(j)
            lane = lax.broadcasted_iota(jnp.int32, (TILE, 128), 1)
            total = jnp.zeros((TILE, 128), F32)
            for pair in range(p.wide // 128):
                here = (pair * 128 + lane) // p.rank == slot
                total = total + jnp.where(here, low[r, pair * 128:(pair + 1) * 128], 0.0)
            low_in[p.n_tp - 1, r] = total
            return carry

        lax.fori_loop(0, p.tiles, body, 0)

    def finish(g):
        if not p.flat:
            all_blocks(g)
        if g == "d":
            pick_low()
            for k in range(p.n_tp - 1):
                low_copy(k).start()
        elif g < p.n_tp - 1:
            sums_copy(g).start()

    def adapter_term():
        for k in range(p.n_tp - 1):
            sums_copy(k).wait_recv()
            low_copy(k).wait_recv()
        row = lax.broadcasted_iota(jnp.int32, (128, p.wide), 0) % p.rank
        col = lax.broadcasted_iota(jnp.int32, (128, p.wide), 1)
        rank_of = (col // p.up_rows) * p.rank_rows + col % p.rank_rows
        spread = jnp.where(row == rank_of, 1.0, 0.0).astype(BF16)

        def body(j, carry):
            r = pl.ds(pl.multiple_of(j * TILE, TILE), TILE)
            slot = slot_at(j)
            total = low_in[p.n_tp - 1, r]
            for k in range(p.n_tp - 1):
                total = total + low_in[k, r]
            laid = jnp.dot(total.astype(BF16), spread, preferred_element_type=F32)
            lane = lax.broadcasted_iota(jnp.int32, (TILE, p.wide), 1)
            here = (lane // p.rank_rows) % p.adapters == slot
            laid = jnp.where(here, laid, 0.0).astype(BF16)
            total = jnp.dot(laid, ubuf[...], preferred_element_type=F32)
            for k in range(p.n_tp - 1):
                total = total + sums_in[k, r]
            term[r] = total
            return carry

        lax.fori_loop(0, p.tiles, body, 0)

    steps = [(g, s) for g in p.groups for s in range(p.nz)]
    final = len(steps) - 1

    def add_up(i):
        g, s = steps[i]
        stage_c(g, s)
        if s == p.nz - 1:
            finish(g)

    ahead_y, ahead_c = LAGS
    own_sends(p.groups[0])
    loads[-1].wait()
    for i, (g, s) in enumerate(steps):
        if i == final:
            add_up(i - ahead_c)
            adapter_term()
        if s > 0:
            stage_z(g, s)
        if s == max(0, p.nz - 2):
            after = p.groups.index(g) + 1
            if after < len(p.groups):
                own_sends(p.groups[after])
        if i >= ahead_y and steps[i - ahead_y][1] > 0:
            stage_y(*steps[i - ahead_y])
        if ahead_c <= i < final:
            add_up(i - ahead_c)
    for i in range(final - ahead_y + 1, final):
        if steps[i][1] > 0:
            stage_y(*steps[i])
    for i in range(final - ahead_c + 1, final):
        add_up(i)
    stage_y(*steps[final])
    add_up(final)

    marks[me] = jnp.full((marks.shape[1], p.lanes), jnp.where(tp == 0, LOWEST, 0.0), F32)
    weight = rel_ref[...]

    def tile_out(j):
        r = pl.ds(pl.multiple_of(j * TILE, TILE), TILE)
        return pltpu.make_async_copy(out.at[r], out_hbm.at[r], out_sem.at[j])

    def last(j, carry):
        r = pl.ds(pl.multiple_of(j * TILE, TILE), TILE)
        adapted = acc[p.n_tp - 1, r] + term[r]
        out[r] = adapted.astype(BF16)
        tile_out(j).start()
        scored = adapted / (1.0 + jnp.exp(-adapted)) * weight
        length = live[j]
        token = lax.broadcasted_iota(jnp.int32, scored.shape, 0)
        scored = jnp.where(token < length, scored, 0.0)
        part = jnp.sum(jnp.sum(scored, axis=0, keepdims=True), axis=1, keepdims=True)
        scale = jnp.sqrt(jnp.full((1, p.lanes), length, jnp.int32).astype(F32))
        slot = doc_slot[passage_doc[j]]
        lane = lax.broadcasted_iota(jnp.int32, (1, p.lanes), 1)
        empty = jnp.where(tp == 0, LOWEST, 0.0)
        marks[me, pl.ds(j, 1)] = jnp.where(lane == slot, part / scale, empty)
        return carry

    lax.fori_loop(0, p.tiles, last, 0)

    def mark_copy(k, slot, sender):
        peer = lax.rem(me + k, devices)
        return pltpu.make_async_remote_copy(
            src_ref=marks.at[slot], dst_ref=marks.at[slot], send_sem=m_send.at[k], recv_sem=m_recv.at[sender],
            device_id={"tp": peer // p.n_owner, "owner": lax.rem(peer, p.n_owner)}, device_id_type=MESH,
        )

    def mark_start(k, carry):
        mark_copy(k, me, me).start()
        return carry

    def mark_wait(k, carry):
        sender = lax.rem(me + k, devices)
        mark_copy(k, sender, sender).wait_recv()
        return carry

    def mark_sent(k, carry):
        mark_copy(k, me, me).wait_send()
        return carry

    lax.fori_loop(1, devices, mark_start, 0)

    for g in p.groups:
        for part in p.part_of[g]:
            for s in range(p.nz):
                def gone(z, upward):
                    if upward:
                        @pl.when(zi + 1 < p.nz)
                        def _():
                            up(part, z).wait_send()
                    if s == 0 or not upward:
                        @pl.when(zi > 0)
                        def _():
                            down(part, z).wait_send()
                    if s > 0:
                        via_twin(s, upward, across(part, z).wait_send)
                    for h in range(2):
                        beside(part, z, ci, h).wait_send()
                if s == 0:
                    gone(zi, True)
                else:
                    each_way(s, gone)
            if p.whole:
                for i, edge in enumerate((0, p.nz - 1)):
                    @pl.when(zi == edge)
                    def _():
                        extra(part, i).wait_send()
    for k in range(p.n_tp - 1):
        sums_copy(k).wait_send()
        low_copy(k).wait_send()

    lax.fori_loop(1, devices, mark_wait, 0)
    best = None
    for o in range(p.n_owner):
        total = marks[o]
        for t in range(1, p.n_tp):
            total = total + marks[t * p.n_owner + o]
        best = total if best is None else jnp.maximum(best, total)
    lane = lax.broadcasted_iota(jnp.int32, best.shape, 1)
    for d in range(p.doc_dev):
        score_ref[d] = jnp.max(jnp.where(lane == owner * p.doc_dev + d, best, 2 * LOWEST))

    lax.fori_loop(1, devices, mark_sent, 0)

    def out_wait(j, carry):
        tile_out(j).wait()
        return carry

    lax.fori_loop(0, p.tiles, out_wait, 0)


def shards(
    n_owner, n_tp,
    tokens,
    base_value_weight,
    adapter_down_factor,
    adapter_up_factor,
    relevance_weight,
    tile_adapter_index,
    adapter_storage_slot,
    tile_live_length,
    passage_document,
    document_output_slot,
):
    p = Plan(
        n_owner, n_tp, tokens, base_value_weight, adapter_down_factor, adapter_up_factor,
        document_output_slot.shape[0],
    )
    if p.flat:
        down = jnp.transpose(adapter_down_factor, (0, 2, 1)).reshape(p.wide, p.rows)
        dshape = (p.n_owner, p.wide, p.rows)
    else:
        down = jnp.transpose(adapter_down_factor, (1, 0, 2)).reshape(p.rows, p.wide)
        dshape = (p.feat, p.wide)
    up = adapter_up_factor.reshape(p.up_rows, p.cols)
    peers = max(1, p.n_tp - 1)
    devices = p.n_tp * p.n_owner
    dma = pltpu.SemaphoreType.DMA
    mark_rows = -(-p.tiles // 8) * 8
    hbm, smem = pl.BlockSpec(memory_space=pl.ANY), pl.BlockSpec(memory_space=pltpu.SMEM)
    return pl.pallas_call(
        functools.partial(kernel, p),
        out_shape=(
            jax.ShapeDtypeStruct((p.tok, p.cols), BF16),
            jax.ShapeDtypeStruct((p.doc_dev,), F32),
        ),
        in_specs=[hbm] * 4 + [pl.BlockSpec(memory_space=pltpu.VMEM)] + [smem] * 5,
        out_specs=(hbm, smem),
        scratch_shapes=[
            pltpu.VMEM((p.tok, p.feat), BF16),
            pltpu.VMEM((p.n_tp, p.feat, p.cols), BF16),
            pltpu.VMEM(dshape, BF16),
            pltpu.VMEM((p.wide, p.cols), BF16),
            pltpu.VMEM((p.n_tp, p.tok, p.cols), F32),
            pltpu.VMEM((p.tok, p.wide), F32),
            pltpu.VMEM((p.n_tp, p.tok, 128), F32),
            pltpu.VMEM((peers, p.tok, p.cols), F32),
            pltpu.VMEM((p.tok, p.cols), F32),
            pltpu.VMEM((p.tok, p.cols), BF16),
            pltpu.VMEM((devices, mark_rows, p.lanes), F32),
            dma((p.n_tp + 3,)),
            dma((p.parts, p.nz)),
            dma((p.parts, p.nz)),
            dma((p.parts, p.nz, 2)),
            dma((p.parts, 2)),
            dma((p.parts, p.nz)),
            dma((p.parts, p.nz)),
            dma((p.parts, p.nz)),
            dma((p.parts, p.nz, 2)),
            dma((p.parts, 2)),
            dma((peers,)),
            dma((peers,)),
            dma((peers,)),
            dma((peers,)),
            dma((devices,)),
            dma((devices,)),
            dma((p.tiles,)),
        ],
        compiler_params=pltpu.CompilerParams(
            collective_id=0, has_side_effects=True, vmem_limit_bytes=60 * 1024 * 1024
        ),
        name="gather_project_score",
    )(
        tokens, base_value_weight, down, up, relevance_weight.reshape(1, p.cols),
        tile_adapter_index, adapter_storage_slot, tile_live_length, passage_document, document_output_slot,
    )


def solution(mesh):
    placed = (
        P(("groups", "owner"), "tp"),
        P(("tp", "owner"), None),
        P(None, ("tp", "owner"), None),
        P(None, "owner", "tp"),
        P("tp"),
        P(("groups", "owner")),
        P(),
        P(("groups", "owner")),
        P(("groups", "owner")),
        P("groups"),
    )
    return jax.shard_map(
        functools.partial(shards, mesh.shape["owner"], mesh.shape["tp"]),
        mesh=mesh,
        in_specs=placed,
        out_specs=(P(("groups", "owner"), "tp"), P(("groups", "owner"))),
        check_vma=False,
    )
```

```python
import functools

import jax
import jax.numpy as jnp
from jax import lax
from jax.experimental import pallas as pl
from jax.experimental.pallas import tpu as pltpu
from jax.sharding import PartitionSpec as P

TILE = 128
CORES = 2
LOWEST = -1e30
LAGS = (1, 2)
MESH = pl.DeviceIdType.MESH
F32 = jnp.float32
BF16 = jnp.bfloat16


class Plan:
    def __init__(self, n_owner, n_tp, tokens, weight, down, up, docs):
        self.n_owner, self.n_tp = n_owner, n_tp
        self.nz = n_owner // CORES
        self.tok, self.feat = tokens.shape
        self.tiles = self.tok // TILE
        self.rows = weight.shape[0]
        self.cols = weight.shape[1] // n_tp
        self.adapters, _, self.rank = down.shape
        self.wide = self.adapters * self.rank
        self.rank_rows = up.shape[1]
        self.up_rows = self.adapters * self.rank_rows
        self.docs = docs
        self.doc_dev = docs // n_owner
        self.lanes = -(-docs // 128) * 128
        self.flat = self.rows % 128 == 0
        self.parts_w = {g: (4 if g == n_tp - 1 else 2) if self.rows >= 256 else 1 for g in range(n_tp)}
        self.parts_d = 2 if self.flat else 1
        self.whole = self.nz >= 4
        self.groups = list(range(n_tp - 1)) + ["d", n_tp - 1]
        self.part_of, self.parts = {}, 0
        for g in self.groups:
            count = self.parts_d + 1 if g == "d" else self.parts_w[g]
            self.part_of[g] = list(range(self.parts, self.parts + count))
            self.parts += count


def kernel(
    p,
    tok_hbm, w_hbm, d_hbm, u_hbm, rel_ref, tile_adapter, storage, live, passage_doc, doc_slot,
    out_hbm, score_ref,
    tok, wbuf, dbuf, ubuf, acc, low, low_in, sums_in, term, out, marks,
    load_sem, z_recv, y_recv, c_recv, e_recv, up_send, down_send, y_send, c_send, e_send,
    x_send, x_recv, l_send, l_recv, m_send, m_recv, out_sem,
):
    gi, owner, tp = lax.axis_index("groups"), lax.axis_index("owner"), lax.axis_index("tp")
    zi, ci = owner // CORES, owner % CORES
    devices = p.n_tp * p.n_owner
    me = tp * p.n_owner + owner

    barrier = pltpu.get_barrier_semaphore()

    def greet(**device):
        pl.semaphore_signal(barrier, inc=1, device_id=device, device_id_type=MESH)

    @pl.when(zi + 1 < p.nz)
    def _():
        greet(owner=lax.rem(owner + CORES, p.n_owner))

    @pl.when(zi > 0)
    def _():
        greet(owner=lax.rem(owner + p.n_owner - CORES, p.n_owner))

    greet(groups=1 - gi)
    greet(owner=zi * CORES + 1 - ci)
    for k in range(p.n_tp - 1):
        greet(tp=lax.rem(tp + 1 + k, p.n_tp))
    met = p.n_tp + 1 + jnp.where(zi > 0, 1, 0) + jnp.where(zi + 1 < p.nz, 1, 0)

    def columns(g):
        t = lax.rem(tp + 1 + g, p.n_tp)
        return pl.ds(pl.multiple_of(t * p.cols, 128), p.cols)

    own_rows = pl.ds(pl.multiple_of(owner * p.rows, p.rows), p.rows)
    loads, loads_of = [], {}
    for g in p.groups:
        loads_of[g] = [len(loads)] + ([len(loads) + 1] if g == "d" else [])
        if g == "d":
            there = dbuf.at[owner] if p.flat else dbuf.at[own_rows]
            loads.append((d_hbm, there))
            loads.append((u_hbm, ubuf.at[pl.ds(pl.multiple_of(owner * p.up_rows, p.up_rows), p.up_rows)]))
        else:
            loads.append((w_hbm.at[:, columns(g)], wbuf.at[g, own_rows]))
    loads.append((tok_hbm, tok))
    loads = [pltpu.make_async_copy(a, b, load_sem.at[i]) for i, (a, b) in enumerate(loads)]
    for load in loads:
        load.start()
    pl.semaphore_wait(barrier, met)

    def piece(part, z, c, h):
        o = z * CORES + c
        for g in p.groups:
            if part in p.part_of[g]:
                k = p.part_of[g].index(part)
                break
        if g == "d":
            if k == p.parts_d:
                half = p.up_rows // 2
                return ubuf.at[pl.ds(pl.multiple_of(o * p.up_rows + h * half, half), half)]
            if p.flat:
                half = p.wide // 2
                size = half // p.parts_d
                return dbuf.at[o, pl.ds(pl.multiple_of(h * half + k * size, size), size)]
            half = p.rows // 2
            return dbuf.at[pl.ds(pl.multiple_of(o * p.rows + h * half, half), half)]
        half = p.rows // 2
        size = half // p.parts_w[g]
        return wbuf.at[g, pl.ds(pl.multiple_of(o * p.rows + h * half + k * size, size), size)]

    def send(part, z, c, h, send_sem, recv_sem, device):
        ref = piece(part, z, c, h)
        return pltpu.make_async_remote_copy(
            src_ref=ref, dst_ref=ref, send_sem=send_sem, recv_sem=recv_sem,
            device_id=device, device_id_type=MESH,
        )

    def up(part, z):
        return send(part, z, ci, gi, up_send.at[part, z], z_recv.at[part, z],
                    {"owner": lax.rem(owner + CORES, p.n_owner)})

    def down(part, z):
        return send(part, z, ci, gi, down_send.at[part, z], z_recv.at[part, z],
                    {"owner": lax.rem(owner + p.n_owner - CORES, p.n_owner)})

    def across(part, z, h=None):
        return send(part, z, ci, gi if h is None else h, y_send.at[part, z], y_recv.at[part, z],
                    {"groups": 1 - gi})

    def beside(part, z, c, h):
        return send(part, z, c, h, c_send.at[part, z, h], c_recv.at[part, z, h],
                    {"owner": zi * CORES + 1 - ci})

    def extra(part, i):
        step = CORES if i == 0 else p.n_owner - CORES
        return send(part, zi, ci, 1 - gi, e_send.at[part, i], e_recv.at[part, i],
                    {"owner": lax.rem(owner + step, p.n_owner)})

    def extra_in(part, z, i):
        return send(part, z, ci, 1 - gi, e_send.at[part, i], e_recv.at[part, i], {"groups": 1 - gi})

    def own_sends(g):
        for i in loads_of[g]:
            loads[i].wait()
        for part in p.part_of[g]:
            @pl.when(zi + 1 < p.nz)
            def _():
                up(part, zi).start()

            @pl.when(zi > 0)
            def _():
                down(part, zi).start()
            for h in range(2):
                beside(part, zi, ci, h).start()
        if p.whole:
            for i, edge in enumerate((0, p.nz - 1)):
                @pl.when(zi == edge)
                def _():
                    for part in p.part_of[g]:
                        extra(part, i).start()

    def each_way(s, body):
        @pl.when(zi - s >= 0)
        def _():
            body(zi - s, True)

        @pl.when(zi + s < p.nz)
        def _():
            body(zi + s, False)

    def via_twin(s, upward, body, other=None):
        if not (p.whole and s == 1):
            body()
            return
        straight = zi == (1 if upward else p.nz - 2)

        @pl.when(jnp.logical_not(straight))
        def _():
            body()
        if other is not None:
            @pl.when(straight)
            def _():
                other()

    def stage_z(g, s):
        def body(z, upward):
            for part in p.part_of[g]:
                up(part, z).wait_recv()
                if upward:
                    @pl.when(zi + 1 < p.nz)
                    def _():
                        up(part, z).start()
                else:
                    @pl.when(zi > 0)
                    def _():
                        down(part, z).start()
                via_twin(s, upward, across(part, z).start)
                beside(part, z, ci, gi).start()
        each_way(s, body)

    def stage_y(g, s):
        def body(z, upward):
            for part in p.part_of[g]:
                via_twin(s, upward, lambda: across(part, z, 1 - gi).wait_recv(),
                         lambda: extra_in(part, z, 0 if upward else 1).wait_recv())
                beside(part, z, ci, 1 - gi).start()
        each_way(s, body)

    def slot_of(g):
        return p.n_tp if g == "d" else g

    def add_block(g, z, first):
        span = CORES * p.rows
        rows = TILE

        def body(j, carry):
            r = pl.ds(pl.multiple_of(j * rows, rows), rows)
            if g == "d":
                total = None
                for c in range(CORES):
                    f = pl.ds(pl.multiple_of(z * span + c * p.rows, 128), p.rows)
                    part = lax.dot_general(tok[r, f], dbuf[z * CORES + c], (((1,), (1,)), ((), ())),
                                           preferred_element_type=F32)
                    total = part if total is None else total + part
                low[r] = total if first else low[r] + total
            else:
                f = pl.ds(pl.multiple_of(z * span, 128), span)
                k = pl.ds(pl.multiple_of(z * span, span), span)
                part = jnp.dot(tok[r, f], wbuf[g, k], preferred_element_type=F32)
                acc[g, r] = part if first else acc[g, r] + part
            return carry

        lax.fori_loop(0, p.tiles, body, 0)

    def all_blocks(g):
        def body(j, carry):
            r = pl.ds(pl.multiple_of(j * TILE, TILE), TILE)
            if g == "d":
                low[r] = jnp.dot(tok[r], dbuf[...], preferred_element_type=F32)
            else:
                acc[g, r] = jnp.dot(tok[r], wbuf[g], preferred_element_type=F32)
            return carry

        lax.fori_loop(0, p.tiles, body, 0)

    def stage_c(g, s):
        def body(z, upward):
            for part in p.part_of[g]:
                for h in range(2):
                    beside(part, z, 1 - ci, h).wait_recv()
            if p.flat:
                add_block(g, z, s == 0)
        if s == 0:
            body(zi, True)
        else:
            each_way(s, body)

    def to_tp(ref_src, ref_dst, k, s_sem, r_sem):
        return pltpu.make_async_remote_copy(
            src_ref=ref_src, dst_ref=ref_dst, send_sem=s_sem.at[k], recv_sem=r_sem.at[k],
            device_id={"tp": lax.rem(tp + 1 + k, p.n_tp)}, device_id_type=MESH,
        )

    def sums_copy(k):
        return to_tp(acc.at[k], sums_in.at[k], k, x_send, x_recv)

    def low_copy(k):
        return to_tp(low_in.at[p.n_tp - 1], low_in.at[k], k, l_send, l_recv)

    def slot_at(j):
        return storage[tile_adapter[j]]

    def pick_low():
        def body(j, carry):
            r = pl.ds(pl.multiple_of(j * TILE, TILE), TILE)
            slot = slot_at(j)
            lane = lax.broadcasted_iota(jnp.int32, (TILE, 128), 1)
            total = jnp.zeros((TILE, 128), F32)
            for pair in range(p.wide // 128):
                here = (pair * 128 + lane) // p.rank == slot
                total = total + jnp.where(here, low[r, pair * 128:(pair + 1) * 128], 0.0)
            low_in[p.n_tp - 1, r] = total
            return carry

        lax.fori_loop(0, p.tiles, body, 0)

    def finish(g):
        if not p.flat:
            all_blocks(g)
        if g == "d":
            pick_low()
            for k in range(p.n_tp - 1):
                low_copy(k).start()
        elif g < p.n_tp - 1:
            sums_copy(g).start()

    def adapter_term():
        for k in range(p.n_tp - 1):
            sums_copy(k).wait_recv()
            low_copy(k).wait_recv()
        row = lax.broadcasted_iota(jnp.int32, (128, p.wide), 0) % p.rank
        col = lax.broadcasted_iota(jnp.int32, (128, p.wide), 1)
        rank_of = (col // p.up_rows) * p.rank_rows + col % p.rank_rows
        spread = jnp.where(row == rank_of, 1.0, 0.0).astype(BF16)

        def body(j, carry):
            r = pl.ds(pl.multiple_of(j * TILE, TILE), TILE)
            slot = slot_at(j)
            total = low_in[p.n_tp - 1, r]
            for k in range(p.n_tp - 1):
                total = total + low_in[k, r]
            laid = jnp.dot(total.astype(BF16), spread, preferred_element_type=F32)
            lane = lax.broadcasted_iota(jnp.int32, (TILE, p.wide), 1)
            here = (lane // p.rank_rows) % p.adapters == slot
            laid = jnp.where(here, laid, 0.0).astype(BF16)
            total = jnp.dot(laid, ubuf[...], preferred_element_type=F32)
            for k in range(p.n_tp - 1):
                total = total + sums_in[k, r]
            term[r] = total
            return carry

        lax.fori_loop(0, p.tiles, body, 0)

    steps = [(g, s) for g in p.groups for s in range(p.nz)]
    final = len(steps) - 1

    def add_up(i):
        g, s = steps[i]
        stage_c(g, s)
        if s == p.nz - 1:
            finish(g)

    ahead_y, ahead_c = LAGS
    own_sends(p.groups[0])
    loads[-1].wait()
    for i, (g, s) in enumerate(steps):
        if s > 0:
            stage_z(g, s)
        if s == max(0, p.nz - 2):
            after = p.groups.index(g) + 1
            if after < len(p.groups):
                own_sends(p.groups[after])
        if ahead_c <= i < final:
            add_up(i - ahead_c)
        if i >= ahead_y and steps[i - ahead_y][1] > 0:
            stage_y(*steps[i - ahead_y])
    add_up(final - ahead_c)
    adapter_term()
    for i in range(final - ahead_y + 1, final):
        if steps[i][1] > 0:
            stage_y(*steps[i])
    for i in range(final - ahead_c + 1, final):
        add_up(i)
    stage_y(*steps[final])
    add_up(final)

    marks[me] = jnp.full((marks.shape[1], p.lanes), jnp.where(tp == 0, LOWEST, 0.0), F32)
    weight = rel_ref[...]

    def tile_out(j):
        r = pl.ds(pl.multiple_of(j * TILE, TILE), TILE)
        return pltpu.make_async_copy(out.at[r], out_hbm.at[r], out_sem.at[j])

    def last(j, carry):
        r = pl.ds(pl.multiple_of(j * TILE, TILE), TILE)
        adapted = acc[p.n_tp - 1, r] + term[r]
        out[r] = adapted.astype(BF16)
        tile_out(j).start()
        scored = adapted / (1.0 + jnp.exp(-adapted)) * weight
        length = live[j]
        token = lax.broadcasted_iota(jnp.int32, scored.shape, 0)
        scored = jnp.where(token < length, scored, 0.0)
        part = jnp.sum(jnp.sum(scored, axis=0, keepdims=True), axis=1, keepdims=True)
        scale = jnp.sqrt(jnp.full((1, p.lanes), length, jnp.int32).astype(F32))
        slot = doc_slot[passage_doc[j]]
        lane = lax.broadcasted_iota(jnp.int32, (1, p.lanes), 1)
        empty = jnp.where(tp == 0, LOWEST, 0.0)
        marks[me, pl.ds(j, 1)] = jnp.where(lane == slot, part / scale, empty)
        return carry

    lax.fori_loop(0, p.tiles, last, 0)

    def mark_copy(k, slot, sender):
        peer = lax.rem(me + k, devices)
        return pltpu.make_async_remote_copy(
            src_ref=marks.at[slot], dst_ref=marks.at[slot], send_sem=m_send.at[k], recv_sem=m_recv.at[sender],
            device_id={"tp": peer // p.n_owner, "owner": lax.rem(peer, p.n_owner)}, device_id_type=MESH,
        )

    def mark_start(k, carry):
        mark_copy(k, me, me).start()
        return carry

    def mark_wait(k, carry):
        sender = lax.rem(me + k, devices)
        mark_copy(k, sender, sender).wait_recv()
        return carry

    def mark_sent(k, carry):
        mark_copy(k, me, me).wait_send()
        return carry

    lax.fori_loop(1, devices, mark_start, 0)

    for g in p.groups:
        for part in p.part_of[g]:
            for s in range(p.nz):
                def gone(z, upward):
                    if upward:
                        @pl.when(zi + 1 < p.nz)
                        def _():
                            up(part, z).wait_send()
                    if s == 0 or not upward:
                        @pl.when(zi > 0)
                        def _():
                            down(part, z).wait_send()
                    if s > 0:
                        via_twin(s, upward, across(part, z).wait_send)
                    for h in range(2):
                        beside(part, z, ci, h).wait_send()
                if s == 0:
                    gone(zi, True)
                else:
                    each_way(s, gone)
            if p.whole:
                for i, edge in enumerate((0, p.nz - 1)):
                    @pl.when(zi == edge)
                    def _():
                        extra(part, i).wait_send()
    for k in range(p.n_tp - 1):
        sums_copy(k).wait_send()
        low_copy(k).wait_send()

    lax.fori_loop(1, devices, mark_wait, 0)
    best = None
    for o in range(p.n_owner):
        total = marks[o]
        for t in range(1, p.n_tp):
            total = total + marks[t * p.n_owner + o]
        best = total if best is None else jnp.maximum(best, total)
    lane = lax.broadcasted_iota(jnp.int32, best.shape, 1)
    for d in range(p.doc_dev):
        score_ref[d] = jnp.max(jnp.where(lane == owner * p.doc_dev + d, best, 2 * LOWEST))

    lax.fori_loop(1, devices, mark_sent, 0)

    def out_wait(j, carry):
        tile_out(j).wait()
        return carry

    lax.fori_loop(0, p.tiles, out_wait, 0)


def shards(
    n_owner, n_tp,
    tokens,
    base_value_weight,
    adapter_down_factor,
    adapter_up_factor,
    relevance_weight,
    tile_adapter_index,
    adapter_storage_slot,
    tile_live_length,
    passage_document,
    document_output_slot,
):
    p = Plan(
        n_owner, n_tp, tokens, base_value_weight, adapter_down_factor, adapter_up_factor,
        document_output_slot.shape[0],
    )
    if p.flat:
        down = jnp.transpose(adapter_down_factor, (0, 2, 1)).reshape(p.wide, p.rows)
        dshape = (p.n_owner, p.wide, p.rows)
    else:
        down = jnp.transpose(adapter_down_factor, (1, 0, 2)).reshape(p.rows, p.wide)
        dshape = (p.feat, p.wide)
    up = adapter_up_factor.reshape(p.up_rows, p.cols)
    peers = max(1, p.n_tp - 1)
    devices = p.n_tp * p.n_owner
    dma = pltpu.SemaphoreType.DMA
    mark_rows = -(-p.tiles // 8) * 8
    hbm, smem = pl.BlockSpec(memory_space=pl.ANY), pl.BlockSpec(memory_space=pltpu.SMEM)
    return pl.pallas_call(
        functools.partial(kernel, p),
        out_shape=(
            jax.ShapeDtypeStruct((p.tok, p.cols), BF16),
            jax.ShapeDtypeStruct((p.doc_dev,), F32),
        ),
        in_specs=[hbm] * 4 + [pl.BlockSpec(memory_space=pltpu.VMEM)] + [smem] * 5,
        out_specs=(hbm, smem),
        scratch_shapes=[
            pltpu.VMEM((p.tok, p.feat), BF16),
            pltpu.VMEM((p.n_tp, p.feat, p.cols), BF16),
            pltpu.VMEM(dshape, BF16),
            pltpu.VMEM((p.wide, p.cols), BF16),
            pltpu.VMEM((p.n_tp, p.tok, p.cols), F32),
            pltpu.VMEM((p.tok, p.wide), F32),
            pltpu.VMEM((p.n_tp, p.tok, 128), F32),
            pltpu.VMEM((peers, p.tok, p.cols), F32),
            pltpu.VMEM((p.tok, p.cols), F32),
            pltpu.VMEM((p.tok, p.cols), BF16),
            pltpu.VMEM((devices, mark_rows, p.lanes), F32),
            dma((p.n_tp + 3,)),
            dma((p.parts, p.nz)),
            dma((p.parts, p.nz)),
            dma((p.parts, p.nz, 2)),
            dma((p.parts, 2)),
            dma((p.parts, p.nz)),
            dma((p.parts, p.nz)),
            dma((p.parts, p.nz)),
            dma((p.parts, p.nz, 2)),
            dma((p.parts, 2)),
            dma((peers,)),
            dma((peers,)),
            dma((peers,)),
            dma((peers,)),
            dma((devices,)),
            dma((devices,)),
            dma((p.tiles,)),
        ],
        compiler_params=pltpu.CompilerParams(
            collective_id=0, has_side_effects=True, vmem_limit_bytes=60 * 1024 * 1024
        ),
        name="gather_project_score",
    )(
        tokens, base_value_weight, down, up, relevance_weight.reshape(1, p.cols),
        tile_adapter_index, adapter_storage_slot, tile_live_length, passage_document, document_output_slot,
    )


def solution(mesh):
    placed = (
        P(("groups", "owner"), "tp"),
        P(("tp", "owner"), None),
        P(None, ("tp", "owner"), None),
        P(None, "owner", "tp"),
        P("tp"),
        P(("groups", "owner")),
        P(),
        P(("groups", "owner")),
        P(("groups", "owner")),
        P("groups"),
    )
    return jax.shard_map(
        functools.partial(shards, mesh.shape["owner"], mesh.shape["tp"]),
        mesh=mesh,
        in_specs=placed,
        out_specs=(P(("groups", "owner"), "tp"), P(("groups", "owner"))),
        check_vma=False,
    )
```
